32 devices in a mesh: shard: 4 (over z), heads: 4 (over x, core), tensor: 2 (over y).
Axes of the slice: x: 2, y: 2, z: 4, core: 2. Of those that a mesh axis runs over, the one named last changes fastest.
Arguments:
- tokens: bfloat16 [4096, 1088], P(('shard', 'heads', 'tensor')), may hold values from -6 to 6
- cotangent: bfloat16 [4096, 1088], P(('shard', 'heads')), may hold values from -6 to 6
- cut_pos: int32 [4], replicated, may hold values from 768 to 1023, as said below
- attend_weight: bfloat16 [1088, 3264], P(('shard', 'tensor')), may hold values from -0.1875 to 0.1875
- out_weight: bfloat16 [1088, 1088], P(('shard', 'tensor')), may hold values from -3 to 3
- up_weight: bfloat16 [1088, 4352], P(None, ('shard', 'tensor')), may hold values from -0.1875 to 0.1875
- down_weight: bfloat16 [4352, 1088], P(('shard', 'tensor')), may hold values from -0.09375 to 0.09375
- first_gain: bfloat16 [1088], P(('shard', 'tensor')), may hold values from 0.5 to 1.5
- first_bias: bfloat16 [1088], P(('shard', 'tensor')), may hold values from -1.5 to 1.5
- query_bias: bfloat16 [1088], P(('shard', 'tensor')), may hold values from -1.5 to 1.5
- value_bias: bfloat16 [1088], P(('shard', 'tensor')), may hold values from -1.5 to 1.5
- out_bias: bfloat16 [1088], P(('shard', 'tensor')), may hold values from -1.5 to 1.5
- second_gain: bfloat16 [1088], P(('shard', 'tensor')), may hold values from 0.5 to 1.5
- second_bias: bfloat16 [1088], P(('shard', 'tensor')), may hold values from -1.5 to 1.5
- up_bias: bfloat16 [4352], P(('shard', 'tensor')), may hold values from -1.5 to 1.5
- down_bias: bfloat16 [1088], P(('shard', 'tensor')), may hold values from -1.5 to 1.5
Outputs:
- layer_out: bfloat16 [4096, 1088], P(('shard', 'heads', 'tensor'))
- tokens_grad: float32 [4096, 1088], P(('shard', 'heads', 'tensor'))
- attend_weight_grad: float32 [1088, 3264], P(('shard', 'tensor'))
- out_weight_grad: float32 [1088, 1088], P(('shard', 'tensor'))
- up_weight_grad: float32 [1088, 4352], P(None, ('shard', 'tensor'))
- down_weight_grad: float32 [4352, 1088], P(('shard', 'tensor'))
- first_gain_grad: float32 [1088], P(('shard', 'tensor'))
- first_bias_grad: float32 [1088], P(('shard', 'tensor'))
- query_bias_grad: float32 [1088], P(('shard', 'tensor'))
- value_bias_grad: float32 [1088], P(('shard', 'tensor'))
- out_bias_grad: float32 [1088], P(('shard', 'tensor'))
- second_gain_grad: float32 [1088], P(('shard', 'tensor'))
- second_bias_grad: float32 [1088], P(('shard', 'tensor'))
- up_bias_grad: float32 [4352], P(('shard', 'tensor'))
- down_bias_grad: float32 [1088], P(('shard', 'tensor'))
The draws below stay inside these ranges and needn't reach their ends.
Inputs may be any that keep to these rules, and one draw needn't show every extreme that they name: cut_pos[s] is the offset within the 1024 tokens of group s at which a new sequence begins; every other token continues the sequence of the token before it, and the very first token begins one. So no sequence spans more than two groups.
All inputs are finite; a program needn't handle non-finite values.
Results may differ from the reference program's by a relative error of at most 0.015.
Values may be sent and summed in bfloat16 or wider, within the bound.
A program may use at most 192 MiB of HBM per device.

```python
import jax
import jax.numpy as jnp
from jax import lax

NH = 17
HD = 64
D = 1088
FF = 4352
GROUP_TOK = 1024
PREV = 256
KEYS = 1280
TOKENS = 4096
N_SHARD = 4


def draw_cut_pos(key, part):
    key = jax.random.fold_in(key, 5)
    key_cut, key_pick = jax.random.split(key)
    cut_values = jax.random.randint(key_cut, (N_SHARD,), GROUP_TOK - PREV, GROUP_TOK)
    first_group = jax.random.randint(key_pick, (), 0, N_SHARD - 1)
    group_ids = jnp.arange(N_SHARD)
    cut_values = jnp.where(group_ids == first_group, GROUP_TOK - PREV, cut_values)
    cut_values = jnp.where(group_ids == first_group + 1, GROUP_TOK - 1, cut_values)
    return cut_values.astype(jnp.int32)


def block_levels(rng, dims, cuts, smallest, high):
    level, own = 1.0, jax.random.fold_in(rng, 6)
    for position, blocks in cuts:
        steps = jnp.exp(jax.random.uniform(jax.random.fold_in(own, position), (blocks,), jnp.float32, smallest / len(cuts), high / len(cuts)))
        level = level * jnp.repeat(steps, dims[position] // blocks).reshape([-1 if axis == position else 1 for axis in range(len(dims))])
    return level


def gaussian(stream_key, dims, scale, reach, shards=(), kind=jnp.bfloat16):
    entries = scale * jax.random.normal(stream_key, dims, jnp.float32)
    if shards:
        entries = entries * block_levels(stream_key, dims, shards, -0.22, 0.18)
    return jnp.clip(entries, -reach, reach).astype(kind)


def setup_inputs(seed: int = 0) -> dict:
    splits = jax.random.split(jax.random.key(seed), 17)
    tokens = gaussian(splits[0], (TOKENS, D), 1.0, 6.0, ((0, 32),))
    cotangent = gaussian(splits[1], (TOKENS, D), 1.0, 6.0, ((0, 16),))
    cut_pos = draw_cut_pos(jax.random.fold_in(splits[16], 71), 0)
    attend_weight = gaussian(splits[3], (D, 3 * D), D ** -0.5, 0.1875, ((0, 8),))
    out_weight = gaussian(splits[4], (D, D), (max(D // 256, 4)) ** -0.5, 3.0, ((0, 8),))
    up_weight = gaussian(splits[5], (D, FF), D ** -0.5, 0.1875, ((1, 8),))
    down_weight = gaussian(splits[6], (FF, D), FF ** -0.5, 0.09375, ((0, 8),))
    first_gain = jnp.clip(1.0 + 0.1 * jax.random.normal(splits[7], (D,), jnp.float32), 0.5, 1.5).astype(jnp.bfloat16)
    first_bias = gaussian(splits[8], (D,), 0.3, 1.5, ((0, 8),))
    query_bias = gaussian(splits[9], (D,), 0.3, 1.5, ((0, 8),))
    value_bias = gaussian(splits[10], (D,), 0.3, 1.5, ((0, 8),))
    out_bias = gaussian(splits[11], (D,), 0.3, 1.5, ((0, 8),))
    second_gain = jnp.clip(1.0 + 0.1 * jax.random.normal(splits[12], (D,), jnp.float32), 0.5, 1.5).astype(jnp.bfloat16)
    second_bias = gaussian(splits[13], (D,), 0.3, 1.5, ((0, 8),))
    up_bias = gaussian(splits[14], (FF,), 0.3, 1.5, ((0, 8),))
    down_bias = gaussian(splits[15], (D,), 0.3, 1.5, ((0, 8),))
    return dict(tokens=tokens, cotangent=cotangent, cut_pos=cut_pos, attend_weight=attend_weight, out_weight=out_weight, up_weight=up_weight, down_weight=down_weight, first_gain=first_gain, first_bias=first_bias, query_bias=query_bias, value_bias=value_bias, out_bias=out_bias, second_gain=second_gain, second_bias=second_bias, up_bias=up_bias, down_bias=down_bias)


EPS = 1e-05
NEG = -1e+30

@jax.custom_vjp
def low(v):
    return lax.optimization_barrier(v.astype(jnp.bfloat16)).astype(jnp.float32)

@jax.custom_vjp
def low_back(v):
    return v

def low_keep(v):
    return (low(v), None)

def low_pass(kept, grad):
    return (grad,)

def back_keep(v):
    return (v, None)

def back_low(kept, grad):
    return (low(grad),)
low.defvjp(low_keep, low_pass)
low_back.defvjp(back_keep, back_low)

def matmul(left, right):
    return jnp.dot(left, right, precision=lax.Precision.HIGHEST, preferred_element_type=jnp.float32)

def layer_norm(values, gain_vec, shift_vec):
    center = values - lax.optimization_barrier(jnp.mean(values, axis=-1, keepdims=True))
    spread = lax.optimization_barrier(jnp.mean(center * center, axis=-1, keepdims=True))
    return center * lax.rsqrt(spread + EPS) * gain_vec + shift_vec

def attend_group(block_items):
    query_rows, key_own, value_own, key_prev, value_prev, group_idx, cut_here, cut_before = block_items
    key_rows = jnp.concatenate([key_prev, key_own], axis=0)
    value_rows = jnp.concatenate([value_prev, value_own], axis=0)
    local_query = jnp.arange(GROUP_TOK, dtype=jnp.int32)
    local_key = jnp.arange(KEYS, dtype=jnp.int32) - PREV
    earlier_start = jnp.where(group_idx > 0, cut_before - GROUP_TOK, 0).astype(jnp.int32)
    seq_start = jnp.where(local_query >= cut_here, cut_here, earlier_start)
    allowed = (local_key[None, :] >= seq_start[:, None]) & (local_key[None, :] <= local_query[:, None])
    scores = jnp.einsum('qhd,khd->hqk', query_rows, key_rows, precision=lax.Precision.HIGHEST) * HD ** (-0.5)
    scores = low_back(scores)
    scores = jnp.where(allowed[None], scores, NEG)
    weights = low(jax.nn.softmax(scores, axis=-1))
    return jnp.einsum('hqk,khd->qhd', weights, value_rows, precision=lax.Precision.HIGHEST)

def reference(tokens, cotangent, cut_pos, attend_weight, out_weight, up_weight, down_weight, first_gain, first_bias, query_bias, value_bias, out_bias, second_gain, second_bias, up_bias, down_bias):
    cut_now = cut_pos.astype(jnp.int32)
    cut_prior = jnp.concatenate([cut_now[:1], cut_now[:-1]]).astype(jnp.int32)

    def forward(token_rows, w_attend, w_out, w_up, w_down, gain_one, shift_one, bias_query, bias_value, bias_out, gain_two, shift_two, bias_up, bias_down):
        normed = low(layer_norm(token_rows, gain_one, shift_one))
        bias_all = jnp.concatenate([bias_query, jnp.zeros_like(bias_query), bias_value])
        projected = low(low_back(matmul(normed, w_attend) + bias_all))
        per_group = projected.reshape(N_SHARD, GROUP_TOK, 3, NH, HD)
        query_rows = per_group[:, :, 0]
        key_own = per_group[:, :, 1]
        value_own = per_group[:, :, 2]
        filler = jnp.zeros((1, PREV, NH, HD), jnp.float32)
        key_prev = jnp.concatenate([filler, key_own[:-1, GROUP_TOK - PREV:]], axis=0)
        value_prev = jnp.concatenate([filler, value_own[:-1, GROUP_TOK - PREV:]], axis=0)
        group_ids = jnp.arange(N_SHARD, dtype=jnp.int32)
        attended = lax.map(jax.checkpoint(attend_group), (query_rows, key_own, value_own, key_prev, value_prev, group_ids, cut_now, cut_prior))
        attended = low(low_back(attended.reshape(TOKENS, D)))
        branch = low_back(matmul(attended, w_out) + bias_out)
        resid = token_rows + branch
        normed_two = low(layer_norm(resid, gain_two, shift_two))

        def feed(rows_in):
            hidden_pre = low_back(matmul(rows_in, w_up) + bias_up)
            hidden_act = low(jax.nn.gelu(hidden_pre, approximate=True))
            return matmul(hidden_act, w_down) + bias_down
        fed_rows = lax.map(jax.checkpoint(feed), normed_two.reshape(N_SHARD, GROUP_TOK, D))
        return resid + fed_rows.reshape(TOKENS, D)
    floats = [array_in.astype(jnp.float32) for array_in in (tokens, attend_weight, out_weight, up_weight, down_weight, first_gain, first_bias, query_bias, value_bias, out_bias, second_gain, second_bias, up_bias, down_bias)]
    result, pullback = jax.vjp(forward, *floats)
    grads = pullback(cotangent.astype(jnp.float32))
    return (result.astype(jnp.bfloat16), grads[0], grads[1], grads[2], grads[3], grads[4], grads[5], grads[6], grads[7], grads[8], grads[9], grads[10], grads[11], grads[12], grads[13])
```

```python
import jax
import jax.numpy as jnp
from jax import lax
from jax.sharding import PartitionSpec as P

NH = 17
HD = 64
SLOTS = 3


EPS = 1e-05
NEG = -1e30


def from_behind(value, axis, steps):
    count = lax.axis_size(axis)
    leading, last = (max(0, -steps), min(count, count - steps))
    return lax.ppermute(value, axis, [(source, source + steps) for source in range(leading, last)])


def layer_norm(values, gain_vec, shift_vec):
    center = values - jnp.mean(values, axis=-1, keepdims=True)
    spread = jnp.mean(center * center, axis=-1, keepdims=True)
    return center * lax.rsqrt(spread + EPS) * gain_vec + shift_vec


def gelu_tanh(values):
    return jax.nn.gelu(values, approximate=True)


def block_scores(query_part, key_rows, bounds, first_query, prev_tok):
    scores = jnp.einsum("qhd,khd->hqk", query_part, key_rows, preferred_element_type=jnp.float32)
    local_query = first_query + jnp.arange(query_part.shape[0], dtype=jnp.int32)
    local_key = jnp.arange(key_rows.shape[0], dtype=jnp.int32) - prev_tok
    start = jnp.where(local_query >= bounds[0], bounds[0], bounds[1])
    allowed = (local_key[None, :] >= start[:, None]) & (local_key[None, :] <= local_query[:, None])
    return jnp.where(allowed[None], scores * HD ** (-0.5), NEG)


def attend(query_flat, key_flat, value_flat, bounds, prev_tok):
    group_tok = query_flat.shape[0]
    block = group_tok // 2
    results, totals = [], []
    for first in range(0, group_tok, block):
        last_key = first + block + prev_tok
        query_part = query_flat[first : first + block].reshape(block, SLOTS, HD)
        key_rows = key_flat[:last_key].reshape(last_key, SLOTS, HD)
        value_rows = value_flat[:last_key].reshape(last_key, SLOTS, HD)
        scores = block_scores(query_part, key_rows, bounds, first, prev_tok)
        row_max = jnp.max(scores, axis=-1, keepdims=True)
        exp_scores = jnp.exp(scores - row_max)
        row_total = jnp.sum(exp_scores, axis=-1, keepdims=True)
        weights = (exp_scores / row_total).astype(jnp.bfloat16)
        result = jnp.einsum("hqk,khd->qhd", weights, value_rows, preferred_element_type=jnp.float32)
        results.append(result.astype(jnp.bfloat16).reshape(block, SLOTS * HD))
        totals.append((row_max + jnp.log(row_total))[..., 0])
    return jnp.concatenate(results, axis=0), totals


def attend_back(query_flat, key_flat, value_flat, d_flat, totals, bounds, prev_tok):
    group_tok = query_flat.shape[0]
    block = group_tok // 2
    key_grad, value_grad, query_grads = 0.0, 0.0, []
    for step, first in enumerate(range(0, group_tok, block)):
        last_key = first + block + prev_tok
        rest = key_flat.shape[0] - last_key
        query_part = query_flat[first : first + block].reshape(block, SLOTS, HD)
        d_part = d_flat[first : first + block].reshape(block, SLOTS, HD)
        key_rows = key_flat[:last_key].reshape(last_key, SLOTS, HD)
        value_rows = value_flat[:last_key].reshape(last_key, SLOTS, HD)
        scores = block_scores(query_part, key_rows, bounds, first, prev_tok)
        probs = jnp.exp(scores - totals[step][..., None])
        d_probs = jnp.einsum("qhd,khd->hqk", d_part, value_rows, preferred_element_type=jnp.float32)
        row_inner = jnp.sum(probs * d_probs, axis=-1, keepdims=True)
        d_scores = (probs * (d_probs - row_inner)).astype(jnp.bfloat16)
        query_grads.append(
            jnp.einsum("hqk,khd->qhd", d_scores, key_rows, preferred_element_type=jnp.float32)
            .reshape(block, SLOTS * HD)
            * HD ** (-0.5)
        )
        part = jnp.einsum("hqk,qhd->khd", d_scores, query_part, preferred_element_type=jnp.float32)
        key_grad += jnp.pad(part.reshape(last_key, SLOTS * HD) * HD ** (-0.5), ((0, rest), (0, 0)))
        part = jnp.einsum(
            "hqk,qhd->khd", probs.astype(jnp.bfloat16), d_part, preferred_element_type=jnp.float32
        )
        value_grad += jnp.pad(part.reshape(last_key, SLOTS * HD), ((0, rest), (0, 0)))
    return jnp.concatenate(query_grads, axis=0), key_grad, value_grad


TEAM = ("heads", "tensor")
OWNERS = ("shard", "tensor")


def set_bounds(group_total, tensor_total):
    base_count, extra_count = NH // group_total, NH % group_total
    firsts, counts = [], []
    next_head = 0
    for group_idx in range(group_total):
        group_size = base_count + (1 if group_idx < extra_count else 0)
        larger = -(-group_size // tensor_total)
        for tensor_pos in range(tensor_total):
            filled = max(0, min(larger, group_size - tensor_pos * larger))
            firsts.append(next_head)
            counts.append(filled)
            next_head += filled
    return firsts, counts


def team_sum(values):
    return lax.psum_scatter(
        values.astype(jnp.bfloat16), TEAM, scatter_dimension=0, tiled=True
    ).astype(jnp.float32)


def swap_team(values):
    return lax.all_to_all(values, TEAM, split_axis=0, concat_axis=0, tiled=True)


def dot_nt(left, right):
    return lax.dot_general(
        left, right, (((1,), (1,)), ((), ())), preferred_element_type=jnp.float32
    )


def dot_tn(left, right):
    return lax.dot_general(
        left, right, (((0,), (0,)), ((), ())), preferred_element_type=jnp.float32
    )


def shards(
    tokens,
    cotangent,
    cut_pos,
    attend_weight,
    out_weight,
    up_weight,
    down_weight,
    first_gain,
    first_bias,
    query_bias,
    value_bias,
    out_bias,
    second_gain,
    second_bias,
    up_bias,
    down_bias,
):
    tok_rows, width = tokens.shape
    heads_count = lax.axis_size("heads")
    tensor_count = lax.axis_size("tensor")
    shard_count = lax.axis_size("shard")
    team = heads_count * tensor_count
    group_tok = tok_rows * team
    prev_tok = group_tok // 4
    key_count = group_tok + prev_tok
    score_scale = HD ** (-0.5)
    slot_width = SLOTS * HD
    shard_idx = lax.axis_index("shard")
    heads_idx = lax.axis_index("heads")
    tensor_idx = lax.axis_index("tensor")
    set_idx = heads_idx * tensor_count + tensor_idx
    firsts, counts = set_bounds(heads_count, tensor_count)
    first_table = jnp.array(firsts, jnp.int32)
    count_table = jnp.array(counts, jnp.int32)
    my_first = first_table[set_idx]
    my_count = count_table[set_idx]
    slot_valid = jnp.arange(SLOTS) < my_count
    group_first = first_table[heads_idx * tensor_count]
    group_heads = max(
        sum(counts[g * tensor_count : (g + 1) * tensor_count]) for g in range(heads_count)
    )
    group_span = max(
        firsts[j] - firsts[j // tensor_count * tensor_count] + SLOTS for j in range(team)
    )
    group_span = max(group_span, group_heads)
    padded_heads = max(max(firsts) + SLOTS, max(firsts[::tensor_count]) + group_span, NH)
    own_rows = attend_weight.shape[0]
    hidden_own = up_weight.shape[1]
    hidden_part = hidden_own // heads_count

    cut_columns = 3 * group_span * HD
    per_head = jnp.pad(
        attend_weight.reshape(own_rows, 3, NH, HD),
        ((0, 0), (0, 0), (0, padded_heads - NH), (0, 0)),
    )
    group_part = lax.dynamic_slice_in_dim(per_head, group_first, group_span, 2)
    vectors = jnp.concatenate(
        [
            first_gain,
            first_bias,
            query_bias,
            value_bias,
            out_bias,
            second_gain,
            second_bias,
            down_bias,
            up_bias,
        ]
    )
    vector_rows = -(-vectors.shape[0] // cut_columns)
    vectors = jnp.pad(vectors, (0, vector_rows * cut_columns - vectors.shape[0]))
    packed = jnp.concatenate(
        [group_part.reshape(own_rows, cut_columns), vectors.reshape(vector_rows, cut_columns)],
        axis=0,
    )
    token_all = lax.all_gather(tokens, TEAM, axis=0, tiled=True)
    packed_all = lax.all_gather(packed, OWNERS, axis=0, tiled=False)
    vector_all = packed_all[:, own_rows:].reshape(shard_count * tensor_count, -1)
    (
        gain_one,
        shift_one,
        bias_query,
        bias_value,
        bias_out,
        gain_two,
        shift_two,
        bias_down,
    ) = (
        vector_all[:, member * own_rows : (member + 1) * own_rows]
        .reshape(width)
        .astype(jnp.float32)
        for member in range(8)
    )
    bias_up = vector_all[:, 8 * own_rows : 8 * own_rows + hidden_own].reshape(
        shard_count, tensor_count, heads_count, hidden_part
    )
    bias_up = lax.dynamic_slice(
        bias_up, (0, tensor_idx, heads_idx, 0), (shard_count, 1, 1, hidden_part)
    ).reshape(shard_count * hidden_part)
    w_set = lax.dynamic_slice_in_dim(
        packed_all[:, :own_rows].reshape(width, 3, group_span, HD), my_first - group_first, SLOTS, 2
    )
    w_set = jnp.where(slot_valid[None, None, :, None], w_set, 0).reshape(width, 3 * slot_width)

    def set_vector(vector):
        slots = jnp.pad(vector.reshape(NH, HD), ((0, padded_heads - NH), (0, 0)))
        slots = lax.dynamic_slice_in_dim(slots, my_first, SLOTS, 0)
        return jnp.where(slot_valid[:, None], slots, 0).reshape(slot_width)

    bias_set = jnp.concatenate(
        [set_vector(bias_query), jnp.zeros((slot_width,), jnp.float32), set_vector(bias_value)]
    )
    w_out = lax.all_gather(out_weight, OWNERS, axis=0, tiled=False).reshape(width, width)
    feed_part = jnp.concatenate(
        [
            lax.dynamic_slice_in_dim(up_weight, heads_idx * hidden_part, hidden_part, 1).T,
            lax.dynamic_slice_in_dim(down_weight, heads_idx * hidden_part, hidden_part, 0),
        ],
        axis=1,
    )
    feed_all = lax.all_gather(feed_part, "shard", axis=0, tiled=False).reshape(
        shard_count * hidden_part, 2 * width
    )
    w_up, w_down = feed_all[:, :width], feed_all[:, width:]
    grad_all = lax.all_gather(cotangent, "heads", axis=0, tiled=True)

    token_f = token_all.astype(jnp.float32)
    center = token_f - jnp.mean(token_f, axis=-1, keepdims=True)
    inverse = lax.rsqrt(jnp.mean(center * center, axis=-1, keepdims=True) + EPS)
    unit = center * inverse
    normed = (unit * gain_one + shift_one).astype(jnp.bfloat16)
    projected = (
        jnp.dot(normed, w_set, preferred_element_type=jnp.float32) + bias_set
    ).astype(jnp.bfloat16)
    query_flat = projected[:, :slot_width]
    own_pair = projected[:, slot_width:]
    earlier = from_behind(own_pair[group_tok - prev_tok :], "shard", 1)
    pair_rows = jnp.concatenate([earlier, own_pair], axis=0)
    key_flat, value_flat = pair_rows[:, :slot_width], pair_rows[:, slot_width:]
    cut_here = cut_pos[shard_idx]
    cut_before = cut_pos[jnp.maximum(shard_idx - 1, 0)]
    earlier_start = jnp.where(shard_idx > 0, cut_before - group_tok, 0)
    bounds = jnp.stack([cut_here, earlier_start]).astype(jnp.int32)
    attended, log_totals = attend(query_flat, key_flat, value_flat, bounds, prev_tok)
    returned = swap_team(attended.reshape(team, tok_rows, slot_width))
    attn_tok = jnp.concatenate(
        [returned[member, :, : counts[member] * HD] for member in range(team)], axis=1
    )
    own_tok_f = tokens.astype(jnp.float32)
    branch_f = jnp.dot(attn_tok, w_out, preferred_element_type=jnp.float32)
    resid = own_tok_f + branch_f + bias_out
    normed_two_f, norm_two_back = jax.vjp(layer_norm, resid, gain_two, shift_two)
    normed_two = normed_two_f.astype(jnp.bfloat16)

    own_grad_rows = lax.dynamic_slice_in_dim(cotangent, tensor_idx * tok_rows, tok_rows, 0)
    d_act = dot_nt(grad_all, w_down)
    feed_rows = lax.all_gather(normed_two, TEAM, axis=0, tiled=True)
    hidden_pre = dot_nt(feed_rows, w_up) + bias_up.astype(jnp.float32)
    hidden_act_f, gelu_back = jax.vjp(gelu_tanh, hidden_pre)
    hidden_act = hidden_act_f.astype(jnp.bfloat16)
    (d_pre_f,) = gelu_back(d_act)
    d_pre = d_pre_f.astype(jnp.bfloat16)
    d_normed_two = team_sum(jnp.dot(d_pre, w_up, preferred_element_type=jnp.float32))
    partial_out = jnp.dot(hidden_act, w_down, preferred_element_type=jnp.float32)
    fed_rows = team_sum(partial_out)
    layer_out = (resid + fed_rows + bias_down).astype(jnp.bfloat16)
    g_feed = jnp.concatenate([dot_tn(d_pre, feed_rows), dot_tn(hidden_act, grad_all)], axis=1)
    g_bias_up = jnp.sum(d_pre.astype(jnp.float32), axis=0)
    g_feed = lax.psum_scatter(
        g_feed.astype(jnp.bfloat16).reshape(shard_count, hidden_part, 2 * width),
        "shard",
        scatter_dimension=0,
        tiled=False,
    )
    g_feed = lax.all_gather(g_feed, "heads", axis=0, tiled=False).reshape(hidden_own, 2 * width)
    g_up = g_feed[:, :width].T.astype(jnp.float32)
    g_down = g_feed[:, width:].astype(jnp.float32)

    own_grad_f = own_grad_rows.astype(jnp.float32)
    g_bias_down = jnp.sum(own_grad_f, axis=0)
    d_resid_norm, g_gain_two, g_shift_two = norm_two_back(d_normed_two)
    d_resid = own_grad_f + d_resid_norm
    d_branch = d_resid.astype(jnp.bfloat16)
    g_bias_out = jnp.sum(d_branch.astype(jnp.float32), axis=0)
    d_attended = dot_nt(d_branch, w_out).astype(jnp.bfloat16)
    d_sets = jnp.stack(
        [
            jnp.pad(
                d_attended[:, firsts[member] * HD : (firsts[member] + counts[member]) * HD],
                ((0, 0), (0, slot_width - counts[member] * HD)),
            )
            for member in range(team)
        ],
        axis=0,
    )
    d_flat = swap_team(d_sets).reshape(group_tok, slot_width)
    g_out = dot_tn(attn_tok, d_branch)
    g_out = lax.psum_scatter(
        g_out.astype(jnp.bfloat16).reshape(shard_count * tensor_count, own_rows, width),
        OWNERS,
        scatter_dimension=0,
        tiled=False,
    )
    g_out = lax.psum(g_out, "heads").astype(jnp.float32)

    query_grad, key_grad, value_grad = attend_back(
        query_flat, key_flat, value_flat, d_flat, log_totals, bounds, prev_tok
    )
    spill = jnp.concatenate([key_grad[:prev_tok], value_grad[:prev_tok]], axis=1)
    later = from_behind(spill.astype(jnp.bfloat16), "shard", -1).astype(jnp.float32)
    later = jnp.pad(later, ((group_tok - prev_tok, 0), (0, 0)))
    own_grads = jnp.concatenate([key_grad[prev_tok:], value_grad[prev_tok:]], axis=1) + later
    d_projected = jnp.concatenate(
        [query_grad.astype(jnp.bfloat16), own_grads.astype(jnp.bfloat16)], axis=1
    )
    d_normed_part = dot_nt(d_projected, w_set)
    d_normed = team_sum(d_normed_part)
    g_attend = dot_tn(normed, d_projected)
    g_attend = lax.psum_scatter(
        g_attend.astype(jnp.bfloat16).reshape(
            shard_count, tensor_count * own_rows, 3 * slot_width
        ),
        "shard",
        scatter_dimension=0,
        tiled=False,
    )
    g_attend = lax.all_to_all(
        g_attend.reshape(tensor_count, own_rows, 3 * slot_width),
        "tensor",
        split_axis=0,
        concat_axis=0,
        tiled=True,
    )
    g_attend = lax.all_gather(g_attend, "heads", axis=0, tiled=False).reshape(
        team, own_rows, 3, slot_width
    )
    g_attend = jnp.concatenate(
        [
            g_attend[member, :, part, : counts[member] * HD]
            for part in range(3)
            for member in range(team)
        ],
        axis=1,
    ).astype(jnp.float32)

    d_sum = jnp.sum(d_projected.astype(jnp.float32), axis=0)

    def place_vector(vector):
        spread = jnp.zeros((padded_heads, HD), jnp.float32)
        slots = jnp.where(slot_valid[:, None], vector.reshape(SLOTS, HD), 0)
        return lax.dynamic_update_slice_in_dim(spread, slots, my_first, 0)[:NH].reshape(width)

    g_bias_up_all = lax.dynamic_update_slice(
        jnp.zeros((shard_count, tensor_count, heads_count, hidden_part), jnp.float32),
        g_bias_up.reshape(shard_count, 1, 1, hidden_part),
        (0, tensor_idx, heads_idx, 0),
    ).reshape(-1)
    terms = jnp.concatenate(
        [
            jnp.sum(d_normed_part * unit, axis=0),
            jnp.sum(d_normed_part, axis=0),
            place_vector(d_sum[:slot_width]),
            place_vector(d_sum[2 * slot_width :]),
            g_bias_out,
            g_gain_two,
            g_shift_two,
            g_bias_down,
            g_bias_up_all,
        ]
    )
    sums = lax.psum(terms, ("shard", "heads", "tensor"))
    owner = shard_idx * tensor_count + tensor_idx
    (
        s_gain_one,
        s_shift_one,
        s_bias_query,
        s_bias_value,
        s_bias_out,
        s_gain_two,
        s_shift_two,
        s_bias_down,
    ) = (
        lax.dynamic_slice_in_dim(sums, member * width + owner * own_rows, own_rows, 0)
        for member in range(8)
    )
    s_bias_up = lax.dynamic_slice_in_dim(sums, 8 * width + owner * hidden_own, hidden_own, 0)

    own_center = own_tok_f - jnp.mean(own_tok_f, axis=-1, keepdims=True)
    own_inverse = lax.rsqrt(jnp.mean(own_center * own_center, axis=-1, keepdims=True) + EPS)
    own_unit = own_center * own_inverse
    scaled = d_normed * gain_one
    tokens_grad = d_resid + own_inverse * (
        scaled
        - jnp.mean(scaled, axis=-1, keepdims=True)
        - own_unit * jnp.mean(scaled * own_unit, axis=-1, keepdims=True)
    )
    return (
        layer_out,
        tokens_grad,
        g_attend,
        g_out,
        g_up,
        g_down,
        s_gain_one,
        s_shift_one,
        s_bias_query,
        s_bias_value,
        s_bias_out,
        s_gain_two,
        s_shift_two,
        s_bias_up,
        s_bias_down,
    )


def solution(mesh):
    placed = (
        P(("shard", "heads", "tensor"), None),
        P(("shard", "heads"), None),
        P(),
        P(("shard", "tensor"), None),
        P(("shard", "tensor"), None),
        P(None, ("shard", "tensor")),
        P(("shard", "tensor"), None),
        P(("shard", "tensor")),
        P(("shard", "tensor")),
        P(("shard", "tensor")),
        P(("shard", "tensor")),
        P(("shard", "tensor")),
        P(("shard", "tensor")),
        P(("shard", "tensor")),
        P(("shard", "tensor")),
        P(("shard", "tensor")),
    )
    return jax.shard_map(
        shards,
        mesh=mesh,
        in_specs=placed,
        out_specs=(
            P(("shard", "heads", "tensor"), None),
            P(("shard", "heads", "tensor"), None),
            P(("shard", "tensor"), None),
            P(("shard", "tensor"), None),
            P(None, ("shard", "tensor")),
            P(("shard", "tensor"), None),
            P(("shard", "tensor")),
            P(("shard", "tensor")),
            P(("shard", "tensor")),
            P(("shard", "tensor")),
            P(("shard", "tensor")),
            P(("shard", "tensor")),
            P(("shard", "tensor")),
            P(("shard", "tensor")),
            P(("shard", "tensor")),
        ),
        check_vma=False,
    )
```

```python
import functools

import jax
import jax.numpy as jnp
from jax import lax
from jax.experimental import pallas as pl
from jax.experimental.pallas import tpu as pltpu
from jax.sharding import PartitionSpec as P

NH = 17
HD = 64
SLOTS = 3
QUERY_BLOCK = 256


EPS = 1e-05
NEG = -1e30


def from_behind(value, axis, steps):
    count = lax.axis_size(axis)
    leading, last = (max(0, -steps), min(count, count - steps))
    return lax.ppermute(value, axis, [(source, source + steps) for source in range(leading, last)])


def layer_norm(values, gain_vec, shift_vec):
    center = values - jnp.mean(values, axis=-1, keepdims=True)
    spread = jnp.mean(center * center, axis=-1, keepdims=True)
    return center * lax.rsqrt(spread + EPS) * gain_vec + shift_vec


def gelu_tanh(values):
    return jax.nn.gelu(values, approximate=True)


def masked_scores(keys, queries, bounds_ref, first_query, prev_tok):
    scores = dot_nt(keys, queries) * HD ** (-0.5)
    local_query = first_query + lax.broadcasted_iota(jnp.int32, (1, scores.shape[1]), 1)
    local_key = lax.broadcasted_iota(jnp.int32, scores.shape, 0) - prev_tok
    start = jnp.where(local_query >= bounds_ref[0], bounds_ref[0], bounds_ref[1])
    allowed = (local_key >= start) & (local_key <= local_query)
    return jnp.where(allowed, scores, NEG)


def attend_kernel(prev_tok, bounds_ref, query_ref, key_ref, value_ref, out_ref, total_ref):
    group_tok = query_ref.shape[0]
    block = min(QUERY_BLOCK, group_tok)
    for first in range(0, group_tok, block):
        last_key = first + block + prev_tok
        results = []
        for slot in range(SLOTS):
            columns = slice(slot * HD, (slot + 1) * HD)
            scores = masked_scores(
                key_ref[:last_key, columns],
                query_ref[first : first + block, columns],
                bounds_ref,
                first,
                prev_tok,
            )
            row_max = jnp.max(scores, axis=0, keepdims=True)
            exp_scores = jnp.exp(scores - row_max)
            row_total = jnp.sum(exp_scores, axis=0, keepdims=True)
            weights = (exp_scores * (1.0 / row_total)).astype(jnp.bfloat16)
            results.append(dot_tn(value_ref[:last_key, columns], weights))
            total_ref[slot : slot + 1, first : first + block] = row_max + jnp.log(row_total)
        out_ref[first : first + block, :] = jnp.concatenate(results, axis=0).T.astype(out_ref.dtype)


def attend_back_kernel(
    prev_tok,
    bounds_ref,
    query_ref,
    key_ref,
    value_ref,
    d_ref,
    total_ref,
    query_grad_ref,
    key_grad_ref,
    value_grad_ref,
):
    group_tok = query_ref.shape[0]
    block = min(QUERY_BLOCK, group_tok)
    key_grad_ref[...] = jnp.zeros_like(key_grad_ref)
    value_grad_ref[...] = jnp.zeros_like(value_grad_ref)
    for first in range(0, group_tok, block):
        last_key = first + block + prev_tok
        query_grads, key_grads, value_grads = [], [], []
        for slot in range(SLOTS):
            columns = slice(slot * HD, (slot + 1) * HD)
            queries = query_ref[first : first + block, columns]
            d_part = d_ref[first : first + block, columns]
            keys = key_ref[:last_key, columns]
            scores = masked_scores(keys, queries, bounds_ref, first, prev_tok)
            probs = jnp.exp(scores - total_ref[slot : slot + 1, first : first + block])
            d_probs = dot_nt(value_ref[:last_key, columns], d_part)
            row_inner = jnp.sum(probs * d_probs, axis=0, keepdims=True)
            d_scores = (probs * (d_probs - row_inner)).astype(jnp.bfloat16)
            query_grads.append(dot_tn(keys, d_scores) * HD ** (-0.5))
            key_grads.append(
                jnp.dot(d_scores, queries, preferred_element_type=jnp.float32) * HD ** (-0.5)
            )
            value_grads.append(
                jnp.dot(probs.astype(jnp.bfloat16), d_part, preferred_element_type=jnp.float32)
            )
        query_grad_ref[first : first + block, :] = jnp.concatenate(query_grads, axis=0).T.astype(
            query_grad_ref.dtype
        )
        key_grad_ref[:last_key, :] += jnp.concatenate(key_grads, axis=1)
        value_grad_ref[:last_key, :] += jnp.concatenate(value_grads, axis=1)


def local_call(kernel, out_shape, inputs, flops):
    vmem = pl.BlockSpec(memory_space=pltpu.VMEM)
    return pl.pallas_call(
        kernel,
        out_shape=out_shape,
        in_specs=[pl.BlockSpec(memory_space=pltpu.SMEM)] + [vmem] * (len(inputs) - 1),
        out_specs=[vmem] * len(out_shape),
        compiler_params=pltpu.CompilerParams(vmem_limit_bytes=48 * 1024 * 1024),
        cost_estimate=pl.CostEstimate(flops=flops, bytes_accessed=4_000_000, transcendentals=0),
    )(*inputs)


def attend(query_flat, key_flat, value_flat, bounds, prev_tok):
    group_tok, columns = query_flat.shape
    return local_call(
        functools.partial(attend_kernel, prev_tok),
        [
            jax.ShapeDtypeStruct((group_tok, columns), jnp.bfloat16),
            jax.ShapeDtypeStruct((SLOTS, group_tok), jnp.float32),
        ],
        (bounds, query_flat, key_flat, value_flat),
        16 * group_tok * key_flat.shape[0] * columns,
    )


def attend_back(query_flat, key_flat, value_flat, d_flat, totals, bounds, prev_tok):
    group_tok, columns = query_flat.shape
    key_count = key_flat.shape[0]
    return local_call(
        functools.partial(attend_back_kernel, prev_tok),
        [
            jax.ShapeDtypeStruct((group_tok, columns), jnp.bfloat16),
            jax.ShapeDtypeStruct((key_count, columns), jnp.float32),
            jax.ShapeDtypeStruct((key_count, columns), jnp.float32),
        ],
        (bounds, query_flat, key_flat, value_flat, d_flat, totals),
        40 * group_tok * key_count * columns,
    )


TEAM = ("heads", "tensor")
OWNERS = ("shard", "tensor")


def set_bounds(group_total, tensor_total):
    base_count, extra_count = NH // group_total, NH % group_total
    firsts, counts = [], []
    next_head = 0
    for group_idx in range(group_total):
        group_size = base_count + (1 if group_idx < extra_count else 0)
        larger = -(-group_size // tensor_total)
        for tensor_pos in range(tensor_total):
            filled = max(0, min(larger, group_size - tensor_pos * larger))
            firsts.append(next_head)
            counts.append(filled)
            next_head += filled
    return firsts, counts


def swap(values, axes):
    return lax.all_to_all(values, axes, split_axis=0, concat_axis=0, tiled=True)


def gather_parts(values, axes):
    return swap(jnp.broadcast_to(values[None], (lax.axis_size(axes), *values.shape)), axes)


def sum_parts(values, axes):
    return jnp.sum(swap(values, axes).astype(jnp.float32), axis=0)


def team_sum(values):
    team = lax.axis_size(TEAM)
    rows = values.shape[0] // team
    return sum_parts(values.astype(jnp.bfloat16).reshape(team, rows, values.shape[1]), TEAM)


def dot_nt(left, right):
    return lax.dot_general(
        left, right, (((1,), (1,)), ((), ())), preferred_element_type=jnp.float32
    )


def dot_tn(left, right):
    return lax.dot_general(
        left, right, (((0,), (0,)), ((), ())), preferred_element_type=jnp.float32
    )


def shards(
    tokens,
    cotangent,
    cut_pos,
    attend_weight,
    out_weight,
    up_weight,
    down_weight,
    first_gain,
    first_bias,
    query_bias,
    value_bias,
    out_bias,
    second_gain,
    second_bias,
    up_bias,
    down_bias,
):
    tok_rows, width = tokens.shape
    heads_count = lax.axis_size("heads")
    tensor_count = lax.axis_size("tensor")
    shard_count = lax.axis_size("shard")
    team = heads_count * tensor_count
    group_tok = tok_rows * team
    prev_tok = group_tok // 4
    key_count = group_tok + prev_tok
    score_scale = HD ** (-0.5)
    slot_width = SLOTS * HD
    shard_idx = lax.axis_index("shard")
    heads_idx = lax.axis_index("heads")
    tensor_idx = lax.axis_index("tensor")
    set_idx = heads_idx * tensor_count + tensor_idx
    firsts, counts = set_bounds(heads_count, tensor_count)
    first_table = jnp.array(firsts, jnp.int32)
    count_table = jnp.array(counts, jnp.int32)
    my_first = first_table[set_idx]
    my_count = count_table[set_idx]
    column_valid = jnp.arange(slot_width) < my_count * HD
    group_first = first_table[heads_idx * tensor_count]
    group_span = max(
        sum(counts[g * tensor_count : (g + 1) * tensor_count]) for g in range(heads_count)
    )
    tail_heads = max(max(firsts) + SLOTS, max(firsts[::tensor_count]) + group_span, NH) - NH
    own_rows = attend_weight.shape[0]
    hidden_own = up_weight.shape[1]
    hidden_part = hidden_own // heads_count

    span = group_span * HD
    padded_weight = jnp.pad(attend_weight, ((0, 0), (0, tail_heads * HD)))
    packed = jnp.concatenate(
        [
            lax.dynamic_slice_in_dim(padded_weight, part * width + group_first * HD, span, 1)
            for part in range(3)
        ],
        axis=1,
    )
    vectors = jnp.concatenate(
        [
            first_gain,
            first_bias,
            query_bias,
            value_bias,
            out_bias,
            second_gain,
            second_bias,
            down_bias,
            up_bias,
        ]
    )
    token_all = gather_parts(tokens, TEAM).reshape(group_tok, width)
    packed_all = lax.all_gather(packed, OWNERS, axis=0, tiled=True)
    vector_all = gather_parts(vectors, OWNERS)
    (
        gain_one,
        shift_one,
        bias_query,
        bias_value,
        bias_out,
        gain_two,
        shift_two,
        bias_down,
    ) = (
        vector_all[:, member * own_rows : (member + 1) * own_rows]
        .reshape(width)
        .astype(jnp.float32)
        for member in range(8)
    )
    bias_up = vector_all[:, 8 * own_rows : 8 * own_rows + hidden_own].reshape(
        shard_count, tensor_count, heads_count, hidden_part
    )
    bias_up = lax.dynamic_slice(
        bias_up, (0, tensor_idx, heads_idx, 0), (shard_count, 1, 1, hidden_part)
    ).reshape(shard_count * hidden_part)
    packed_all = jnp.pad(packed_all, ((0, 0), (0, slot_width)))
    set_offset = (my_first - group_first) * HD
    w_set = jnp.concatenate(
        [
            jnp.where(
                column_valid,
                lax.dynamic_slice_in_dim(packed_all, part * span + set_offset, slot_width, 1),
                0,
            )
            for part in range(3)
        ],
        axis=1,
    )

    def set_vector(vector):
        padded = jnp.pad(vector, (0, tail_heads * HD))
        return jnp.where(
            column_valid, lax.dynamic_slice_in_dim(padded, my_first * HD, slot_width, 0), 0
        )

    bias_set = jnp.concatenate(
        [set_vector(bias_query), jnp.zeros((slot_width,), jnp.float32), set_vector(bias_value)]
    )
    out_cut = width // heads_count
    w_out = gather_parts(
        lax.all_gather(
            lax.dynamic_slice_in_dim(out_weight, heads_idx * out_cut, out_cut, 1),
            OWNERS,
            axis=0,
            tiled=True,
        ),
        "heads",
    )
    feed_part = jnp.concatenate(
        [
            lax.dynamic_slice_in_dim(up_weight, heads_idx * hidden_part, hidden_part, 1).T,
            lax.dynamic_slice_in_dim(down_weight, heads_idx * hidden_part, hidden_part, 0),
        ],
        axis=1,
    )
    feed_all = lax.all_gather(feed_part, "shard", axis=0, tiled=True)
    w_up, w_down = feed_all[:, :width], feed_all[:, width:]
    grad_all = gather_parts(cotangent, "heads").reshape(group_tok, width)

    token_f = token_all.astype(jnp.float32)
    center = token_f - jnp.mean(token_f, axis=-1, keepdims=True)
    inverse = lax.rsqrt(jnp.mean(center * center, axis=-1, keepdims=True) + EPS)
    unit = center * inverse
    normed = (unit * gain_one + shift_one).astype(jnp.bfloat16)
    projected = (
        jnp.dot(normed, w_set, preferred_element_type=jnp.float32) + bias_set
    ).astype(jnp.bfloat16)
    query_flat = projected[:, :slot_width]
    own_pair = projected[:, slot_width:]
    earlier = from_behind(own_pair[group_tok - prev_tok :], "shard", 1)
    pair_rows = jnp.concatenate([earlier, own_pair], axis=0)
    key_flat, value_flat = pair_rows[:, :slot_width], pair_rows[:, slot_width:]
    cut_here = cut_pos[shard_idx]
    cut_before = cut_pos[jnp.maximum(shard_idx - 1, 0)]
    earlier_start = jnp.where(shard_idx > 0, cut_before - group_tok, 0)
    bounds = jnp.stack([cut_here, earlier_start]).astype(jnp.int32)
    attended, log_totals = attend(query_flat, key_flat, value_flat, bounds, prev_tok)
    returned = swap(attended.reshape(team, tok_rows, slot_width), TEAM)
    attn_tok = jnp.concatenate(
        [returned[member, :, : counts[member] * HD] for member in range(team)], axis=1
    )
    own_tok_f = tokens.astype(jnp.float32)
    branch_f = jnp.concatenate(
        [
            jnp.dot(attn_tok, w_out[member], preferred_element_type=jnp.float32)
            for member in range(heads_count)
        ],
        axis=1,
    )
    resid = own_tok_f + branch_f + bias_out
    normed_two_f, norm_two_back = jax.vjp(layer_norm, resid, gain_two, shift_two)
    normed_two = normed_two_f.astype(jnp.bfloat16)

    own_grad_rows = lax.dynamic_slice_in_dim(cotangent, tensor_idx * tok_rows, tok_rows, 0)
    d_act = dot_nt(grad_all, w_down)
    feed_rows = gather_parts(normed_two, TEAM).reshape(group_tok, width)
    hidden_pre = dot_nt(feed_rows, w_up) + bias_up.astype(jnp.float32)
    hidden_act_f, gelu_back = jax.vjp(gelu_tanh, hidden_pre)
    hidden_act = hidden_act_f.astype(jnp.bfloat16)
    (d_pre_f,) = gelu_back(d_act)
    d_pre = d_pre_f.astype(jnp.bfloat16)
    d_normed_two = team_sum(jnp.dot(d_pre, w_up, preferred_element_type=jnp.float32))
    partial_out = jnp.dot(hidden_act, w_down, preferred_element_type=jnp.float32)
    fed_rows = team_sum(partial_out)
    layer_out = (resid + fed_rows + bias_down).astype(jnp.bfloat16)
    g_feed = jnp.concatenate([dot_tn(d_pre, feed_rows), dot_tn(hidden_act, grad_all)], axis=1)
    g_bias_up = jnp.sum(d_pre.astype(jnp.float32), axis=0)
    g_feed = sum_parts(
        g_feed.astype(jnp.bfloat16).reshape(shard_count, hidden_part, 2 * width), "shard"
    )
    g_feed = gather_parts(g_feed.astype(jnp.bfloat16), "heads").reshape(hidden_own, 2 * width)
    g_up = g_feed[:, :width].T.astype(jnp.float32)
    g_down = g_feed[:, width:].astype(jnp.float32)

    own_grad_f = own_grad_rows.astype(jnp.float32)
    g_bias_down = jnp.sum(own_grad_f, axis=0)
    d_resid_norm, g_gain_two, g_shift_two = norm_two_back(d_normed_two)
    d_resid = own_grad_f + d_resid_norm
    d_branch = d_resid.astype(jnp.bfloat16)
    g_bias_out = jnp.sum(d_branch.astype(jnp.float32), axis=0)
    d_attended = sum(
        dot_nt(d_branch[:, member * out_cut : (member + 1) * out_cut], w_out[member])
        for member in range(heads_count)
    ).astype(jnp.bfloat16)
    d_sets = jnp.stack(
        [
            jnp.pad(
                d_attended[:, firsts[member] * HD : (firsts[member] + counts[member]) * HD],
                ((0, 0), (0, slot_width - counts[member] * HD)),
            )
            for member in range(team)
        ],
        axis=0,
    )
    d_flat = swap(d_sets, TEAM).reshape(group_tok, slot_width)
    g_out = dot_tn(attn_tok, d_branch)
    g_out = sum_parts(
        g_out.astype(jnp.bfloat16).reshape(shard_count * tensor_count, own_rows, width), OWNERS
    )
    g_out = jnp.sum(
        gather_parts(g_out.astype(jnp.bfloat16), "heads").astype(jnp.float32), axis=0
    )

    query_grad, key_grad, value_grad = attend_back(
        query_flat, key_flat, value_flat, d_flat, log_totals, bounds, prev_tok
    )
    spill = jnp.concatenate([key_grad[:prev_tok], value_grad[:prev_tok]], axis=1)
    later = from_behind(spill.astype(jnp.bfloat16), "shard", -1).astype(jnp.float32)
    later = jnp.pad(later, ((group_tok - prev_tok, 0), (0, 0)))
    own_grads = jnp.concatenate([key_grad[prev_tok:], value_grad[prev_tok:]], axis=1) + later
    d_projected = jnp.concatenate(
        [query_grad.astype(jnp.bfloat16), own_grads.astype(jnp.bfloat16)], axis=1
    )
    d_normed_part = dot_nt(d_projected, w_set)
    d_normed = team_sum(d_normed_part)
    g_attend = dot_tn(normed, d_projected)
    g_attend = sum_parts(
        g_attend.astype(jnp.bfloat16).reshape(
            shard_count, tensor_count * own_rows, 3 * slot_width
        ),
        "shard",
    )
    g_attend = g_attend.astype(jnp.bfloat16).reshape(1, tensor_count, own_rows, 3 * slot_width)
    g_attend = swap(
        jnp.broadcast_to(g_attend, (heads_count, *g_attend.shape[1:])).reshape(
            team, own_rows, 3 * slot_width
        ),
        TEAM,
    )
    g_attend = jnp.concatenate(
        [
            g_attend[member, :, part * slot_width : part * slot_width + counts[member] * HD]
            for part in range(3)
            for member in range(team)
        ],
        axis=1,
    ).astype(jnp.float32)

    d_sum = jnp.sum(d_projected.astype(jnp.float32), axis=0)

    def place_vector(vector):
        spread = jnp.zeros((width + tail_heads * HD,), jnp.float32)
        own_terms = jnp.where(column_valid, vector, 0)
        return lax.dynamic_update_slice_in_dim(spread, own_terms, my_first * HD, 0)[:width]

    g_bias_up_all = lax.dynamic_update_slice(
        jnp.zeros((shard_count, tensor_count, heads_count, hidden_part), jnp.float32),
        g_bias_up.reshape(shard_count, 1, 1, hidden_part),
        (0, tensor_idx, heads_idx, 0),
    ).reshape(-1)
    owners = shard_count * tensor_count
    terms = jnp.concatenate(
        [
            vector.reshape(owners, -1)
            for vector in (
                jnp.sum(d_normed_part * unit, axis=0),
                jnp.sum(d_normed_part, axis=0),
                place_vector(d_sum[:slot_width]),
                place_vector(d_sum[2 * slot_width :]),
                g_bias_out,
                g_gain_two,
                g_shift_two,
                g_bias_down,
                g_bias_up_all,
            )
        ],
        axis=1,
    )
    sums = jnp.sum(gather_parts(sum_parts(terms, OWNERS), "heads"), axis=0)
    (
        s_gain_one,
        s_shift_one,
        s_bias_query,
        s_bias_value,
        s_bias_out,
        s_gain_two,
        s_shift_two,
        s_bias_down,
    ) = (sums[member * own_rows : (member + 1) * own_rows] for member in range(8))
    s_bias_up = sums[8 * own_rows :]

    own_center = own_tok_f - jnp.mean(own_tok_f, axis=-1, keepdims=True)
    own_inverse = lax.rsqrt(jnp.mean(own_center * own_center, axis=-1, keepdims=True) + EPS)
    own_unit = own_center * own_inverse
    scaled = d_normed * gain_one
    tokens_grad = d_resid + own_inverse * (
        scaled
        - jnp.mean(scaled, axis=-1, keepdims=True)
        - own_unit * jnp.mean(scaled * own_unit, axis=-1, keepdims=True)
    )
    return (
        layer_out,
        tokens_grad,
        g_attend,
        g_out,
        g_up,
        g_down,
        s_gain_one,
        s_shift_one,
        s_bias_query,
        s_bias_value,
        s_bias_out,
        s_gain_two,
        s_shift_two,
        s_bias_up,
        s_bias_down,
    )


def solution(mesh):
    placed = (
        P(("shard", "heads", "tensor"), None),
        P(("shard", "heads"), None),
        P(),
        P(("shard", "tensor"), None),
        P(("shard", "tensor"), None),
        P(None, ("shard", "tensor")),
        P(("shard", "tensor"), None),
        P(("shard", "tensor")),
        P(("shard", "tensor")),
        P(("shard", "tensor")),
        P(("shard", "tensor")),
        P(("shard", "tensor")),
        P(("shard", "tensor")),
        P(("shard", "tensor")),
        P(("shard", "tensor")),
        P(("shard", "tensor")),
    )
    return jax.shard_map(
        shards,
        mesh=mesh,
        in_specs=placed,
        out_specs=(
            P(("shard", "heads", "tensor"), None),
            P(("shard", "heads", "tensor"), None),
            P(("shard", "tensor"), None),
            P(("shard", "tensor"), None),
            P(None, ("shard", "tensor")),
            P(("shard", "tensor"), None),
            P(("shard", "tensor")),
            P(("shard", "tensor")),
            P(("shard", "tensor")),
            P(("shard", "tensor")),
            P(("shard", "tensor")),
            P(("shard", "tensor")),
            P(("shard", "tensor")),
            P(("shard", "tensor")),
            P(("shard", "tensor")),
        ),
        check_vma=False,
    )
```

```python
import functools

import jax
import jax.numpy as jnp
from jax import lax
from jax.experimental import pallas as pl
from jax.experimental.pallas import tpu as pltpu
from jax.sharding import PartitionSpec as P

NH = 17
HD = 64
SLOTS = 3
QUERY_BLOCK = 256


EPS = 1e-05
NEG = -1e30


def from_behind(value, axis, steps):
    count = lax.axis_size(axis)
    leading, last = (max(0, -steps), min(count, count - steps))
    return lax.ppermute(value, axis, [(source, source + steps) for source in range(leading, last)])


def layer_norm(values, gain_vec, shift_vec):
    center = values - jnp.mean(values, axis=-1, keepdims=True)
    spread = jnp.mean(center * center, axis=-1, keepdims=True)
    return center * lax.rsqrt(spread + EPS) * gain_vec + shift_vec


def gelu_tanh(values):
    return jax.nn.gelu(values, approximate=True)


def masked_scores(keys, queries, bounds_ref, first_query, prev_tok):
    scores = dot_nt(keys, queries) * HD ** (-0.5)
    local_query = first_query + lax.broadcasted_iota(jnp.int32, (1, scores.shape[1]), 1)
    local_key = lax.broadcasted_iota(jnp.int32, scores.shape, 0) - prev_tok
    start = jnp.where(local_query >= bounds_ref[0], bounds_ref[0], bounds_ref[1])
    allowed = (local_key >= start) & (local_key <= local_query)
    return jnp.where(allowed, scores, NEG)


def attend_kernel(prev_tok, bounds_ref, query_ref, key_ref, value_ref, out_ref, total_ref):
    group_tok = query_ref.shape[0]
    block = min(QUERY_BLOCK, group_tok)
    for first in range(0, group_tok, block):
        last_key = first + block + prev_tok
        results = []
        for slot in range(SLOTS):
            columns = slice(slot * HD, (slot + 1) * HD)
            scores = masked_scores(
                key_ref[:last_key, columns],
                query_ref[first : first + block, columns],
                bounds_ref,
                first,
                prev_tok,
            )
            row_max = jnp.max(scores, axis=0, keepdims=True)
            exp_scores = jnp.exp(scores - row_max)
            row_total = jnp.sum(exp_scores, axis=0, keepdims=True)
            weights = (exp_scores * (1.0 / row_total)).astype(jnp.bfloat16)
            results.append(dot_tn(value_ref[:last_key, columns], weights))
            total_ref[slot : slot + 1, first : first + block] = row_max + jnp.log(row_total)
        out_ref[first : first + block, :] = jnp.concatenate(results, axis=0).T.astype(out_ref.dtype)


def attend_back_kernel(
    prev_tok,
    bounds_ref,
    query_ref,
    key_ref,
    value_ref,
    d_ref,
    total_ref,
    query_grad_ref,
    key_grad_ref,
    value_grad_ref,
):
    group_tok = query_ref.shape[0]
    block = min(QUERY_BLOCK, group_tok)
    key_grad_ref[...] = jnp.zeros_like(key_grad_ref)
    value_grad_ref[...] = jnp.zeros_like(value_grad_ref)
    for first in range(0, group_tok, block):
        last_key = first + block + prev_tok
        query_grads, key_grads, value_grads = [], [], []
        for slot in range(SLOTS):
            columns = slice(slot * HD, (slot + 1) * HD)
            queries = query_ref[first : first + block, columns]
            d_part = d_ref[first : first + block, columns]
            keys = key_ref[:last_key, columns]
            scores = masked_scores(keys, queries, bounds_ref, first, prev_tok)
            probs = jnp.exp(scores - total_ref[slot : slot + 1, first : first + block])
            d_probs = dot_nt(value_ref[:last_key, columns], d_part)
            row_inner = jnp.sum(probs * d_probs, axis=0, keepdims=True)
            d_scores = (probs * (d_probs - row_inner)).astype(jnp.bfloat16)
            query_grads.append(dot_tn(keys, d_scores) * HD ** (-0.5))
            key_grads.append(
                jnp.dot(d_scores, queries, preferred_element_type=jnp.float32) * HD ** (-0.5)
            )
            value_grads.append(
                jnp.dot(probs.astype(jnp.bfloat16), d_part, preferred_element_type=jnp.float32)
            )
        query_grad_ref[first : first + block, :] = jnp.concatenate(query_grads, axis=0).T.astype(
            query_grad_ref.dtype
        )
        key_grad_ref[:last_key, :] += jnp.concatenate(key_grads, axis=1)
        value_grad_ref[:last_key, :] += jnp.concatenate(value_grads, axis=1)


def local_call(kernel, out_shape, inputs, flops):
    vmem = pl.BlockSpec(memory_space=pltpu.VMEM)
    return pl.pallas_call(
        kernel,
        out_shape=out_shape,
        in_specs=[pl.BlockSpec(memory_space=pltpu.SMEM)] + [vmem] * (len(inputs) - 1),
        out_specs=[vmem] * len(out_shape),
        compiler_params=pltpu.CompilerParams(vmem_limit_bytes=48 * 1024 * 1024),
        cost_estimate=pl.CostEstimate(flops=flops, bytes_accessed=4_000_000, transcendentals=0),
    )(*inputs)


def attend(query_flat, key_flat, value_flat, bounds, prev_tok):
    group_tok, columns = query_flat.shape
    return local_call(
        functools.partial(attend_kernel, prev_tok),
        [
            jax.ShapeDtypeStruct((group_tok, columns), jnp.bfloat16),
            jax.ShapeDtypeStruct((SLOTS, group_tok), jnp.float32),
        ],
        (bounds, query_flat, key_flat, value_flat),
        16 * group_tok * key_flat.shape[0] * columns,
    )


def attend_back(query_flat, key_flat, value_flat, d_flat, totals, bounds, prev_tok):
    group_tok, columns = query_flat.shape
    key_count = key_flat.shape[0]
    return local_call(
        functools.partial(attend_back_kernel, prev_tok),
        [
            jax.ShapeDtypeStruct((group_tok, columns), jnp.bfloat16),
            jax.ShapeDtypeStruct((key_count, columns), jnp.float32),
            jax.ShapeDtypeStruct((key_count, columns), jnp.float32),
        ],
        (bounds, query_flat, key_flat, value_flat, d_flat, totals),
        40 * group_tok * key_count * columns,
    )


TEAM = ("heads", "tensor")
OWNERS = ("shard", "tensor")


def set_bounds(group_total, tensor_total):
    base_count, extra_count = NH // group_total, NH % group_total
    firsts, counts = [], []
    next_head = 0
    for group_idx in range(group_total):
        group_size = base_count + (1 if group_idx < extra_count else 0)
        larger = -(-group_size // tensor_total)
        for tensor_pos in range(tensor_total):
            filled = max(0, min(larger, group_size - tensor_pos * larger))
            firsts.append(next_head)
            counts.append(filled)
            next_head += filled
    return firsts, counts


def swap(values, axes):
    return lax.all_to_all(values, axes, split_axis=0, concat_axis=0, tiled=True)


def gather_parts(values, axes):
    return swap(jnp.broadcast_to(values[None], (lax.axis_size(axes), *values.shape)), axes)


def sum_parts(values, axes):
    return jnp.sum(swap(values, axes).astype(jnp.float32), axis=0)


def team_sum(values):
    team = lax.axis_size(TEAM)
    rows = values.shape[0] // team
    return sum_parts(values.astype(jnp.bfloat16).reshape(team, rows, values.shape[1]), TEAM)


def dot_nt(left, right):
    return lax.dot_general(
        left, right, (((1,), (1,)), ((), ())), preferred_element_type=jnp.float32
    )


def dot_tn(left, right):
    return lax.dot_general(
        left, right, (((0,), (0,)), ((), ())), preferred_element_type=jnp.float32
    )


def shards(
    tokens,
    cotangent,
    cut_pos,
    attend_weight,
    out_weight,
    up_weight,
    down_weight,
    first_gain,
    first_bias,
    query_bias,
    value_bias,
    out_bias,
    second_gain,
    second_bias,
    up_bias,
    down_bias,
):
    tok_rows, width = tokens.shape
    heads_count = lax.axis_size("heads")
    tensor_count = lax.axis_size("tensor")
    shard_count = lax.axis_size("shard")
    team = heads_count * tensor_count
    group_tok = tok_rows * team
    prev_tok = group_tok // 4
    key_count = group_tok + prev_tok
    score_scale = HD ** (-0.5)
    slot_width = SLOTS * HD
    shard_idx = lax.axis_index("shard")
    heads_idx = lax.axis_index("heads")
    tensor_idx = lax.axis_index("tensor")
    set_idx = heads_idx * tensor_count + tensor_idx
    firsts, counts = set_bounds(heads_count, tensor_count)
    first_table = jnp.array(firsts, jnp.int32)
    count_table = jnp.array(counts, jnp.int32)
    my_first = first_table[set_idx]
    my_count = count_table[set_idx]
    column_valid = jnp.arange(slot_width) < my_count * HD
    group_first = first_table[heads_idx * tensor_count]
    group_span = max(
        sum(counts[g * tensor_count : (g + 1) * tensor_count]) for g in range(heads_count)
    )
    tail_heads = max(max(firsts) + SLOTS, max(firsts[::tensor_count]) + group_span, NH) - NH
    own_rows = attend_weight.shape[0]
    hidden_own = up_weight.shape[1]
    hidden_part = hidden_own // heads_count

    span = group_span * HD
    padded_weight = jnp.pad(attend_weight, ((0, 0), (0, tail_heads * HD)))
    packed = jnp.concatenate(
        [
            lax.dynamic_slice_in_dim(padded_weight, part * width + group_first * HD, span, 1)
            for part in range(3)
        ],
        axis=1,
    )
    vectors = jnp.concatenate(
        [
            first_gain,
            first_bias,
            query_bias,
            value_bias,
            out_bias,
            second_gain,
            second_bias,
            down_bias,
            up_bias,
        ]
    )
    token_all = gather_parts(tokens, TEAM).reshape(group_tok, width)
    packed_all = lax.all_gather(packed, OWNERS, axis=0, tiled=True)
    vector_all = gather_parts(vectors, OWNERS)
    (
        gain_one,
        shift_one,
        bias_query,
        bias_value,
        bias_out,
        gain_two,
        shift_two,
        bias_down,
    ) = (
        vector_all[:, member * own_rows : (member + 1) * own_rows]
        .reshape(width)
        .astype(jnp.float32)
        for member in range(8)
    )
    bias_up = vector_all[:, 8 * own_rows : 8 * own_rows + hidden_own].reshape(
        shard_count, tensor_count, heads_count, hidden_part
    )
    bias_up = lax.dynamic_slice(
        bias_up, (0, tensor_idx, heads_idx, 0), (shard_count, 1, 1, hidden_part)
    ).reshape(shard_count * hidden_part)
    packed_all = jnp.pad(packed_all, ((0, 0), (0, slot_width)))
    set_offset = (my_first - group_first) * HD
    w_set = jnp.concatenate(
        [
            jnp.where(
                column_valid,
                lax.dynamic_slice_in_dim(packed_all, part * span + set_offset, slot_width, 1),
                0,
            )
            for part in range(3)
        ],
        axis=1,
    )

    def set_vector(vector):
        padded = jnp.pad(vector, (0, tail_heads * HD))
        return jnp.where(
            column_valid, lax.dynamic_slice_in_dim(padded, my_first * HD, slot_width, 0), 0
        )

    bias_set = jnp.concatenate(
        [set_vector(bias_query), jnp.zeros((slot_width,), jnp.float32), set_vector(bias_value)]
    )
    w_out = lax.all_gather(out_weight, OWNERS, axis=0, tiled=True)
    feed_part = jnp.concatenate(
        [
            lax.dynamic_slice_in_dim(up_weight, heads_idx * hidden_part, hidden_part, 1).T,
            lax.dynamic_slice_in_dim(down_weight, heads_idx * hidden_part, hidden_part, 0),
        ],
        axis=1,
    )
    feed_all = lax.all_gather(feed_part, "shard", axis=0, tiled=True)
    w_up, w_down = feed_all[:, :width], feed_all[:, width:]
    grad_all = gather_parts(cotangent, "heads").reshape(group_tok, width)

    token_f = token_all.astype(jnp.float32)
    center = token_f - jnp.mean(token_f, axis=-1, keepdims=True)
    inverse = lax.rsqrt(jnp.mean(center * center, axis=-1, keepdims=True) + EPS)
    unit = center * inverse
    normed = (unit * gain_one + shift_one).astype(jnp.bfloat16)
    projected = (
        jnp.dot(normed, w_set, preferred_element_type=jnp.float32) + bias_set
    ).astype(jnp.bfloat16)
    query_flat = projected[:, :slot_width]
    own_pair = projected[:, slot_width:]
    earlier = from_behind(own_pair[group_tok - prev_tok :], "shard", 1)
    pair_rows = jnp.concatenate([earlier, own_pair], axis=0)
    key_flat, value_flat = pair_rows[:, :slot_width], pair_rows[:, slot_width:]
    cut_here = cut_pos[shard_idx]
    cut_before = cut_pos[jnp.maximum(shard_idx - 1, 0)]
    earlier_start = jnp.where(shard_idx > 0, cut_before - group_tok, 0)
    bounds = jnp.stack([cut_here, earlier_start]).astype(jnp.int32)
    attended, log_totals = attend(query_flat, key_flat, value_flat, bounds, prev_tok)
    returned = swap(attended.reshape(team, tok_rows, slot_width), TEAM)
    attn_tok = jnp.concatenate(
        [returned[member, :, : counts[member] * HD] for member in range(team)], axis=1
    )
    own_tok_f = tokens.astype(jnp.float32)
    branch_f = jnp.dot(attn_tok, w_out, preferred_element_type=jnp.float32)
    resid = own_tok_f + branch_f + bias_out
    normed_two_f, norm_two_back = jax.vjp(layer_norm, resid, gain_two, shift_two)
    normed_two = normed_two_f.astype(jnp.bfloat16)

    own_grad_rows = lax.dynamic_slice_in_dim(cotangent, tensor_idx * tok_rows, tok_rows, 0)
    d_act = dot_nt(grad_all, w_down)
    feed_rows = gather_parts(normed_two, TEAM).reshape(group_tok, width)
    hidden_pre = dot_nt(feed_rows, w_up) + bias_up.astype(jnp.float32)
    hidden_act_f, gelu_back = jax.vjp(gelu_tanh, hidden_pre)
    hidden_act = hidden_act_f.astype(jnp.bfloat16)
    (d_pre_f,) = gelu_back(d_act)
    d_pre = d_pre_f.astype(jnp.bfloat16)
    d_normed_two = team_sum(jnp.dot(d_pre, w_up, preferred_element_type=jnp.float32))
    partial_out = jnp.dot(hidden_act, w_down, preferred_element_type=jnp.float32)
    fed_rows = lax.psum_scatter(
        partial_out.astype(jnp.bfloat16), TEAM, scatter_dimension=0, tiled=True
    ).astype(jnp.float32)
    layer_out = (resid + fed_rows + bias_down).astype(jnp.bfloat16)
    g_feed = jnp.concatenate([dot_tn(d_pre, feed_rows), dot_tn(hidden_act, grad_all)], axis=1)
    g_bias_up = jnp.sum(d_pre.astype(jnp.float32), axis=0)
    g_feed = lax.psum_scatter(
        g_feed.astype(jnp.bfloat16).reshape(shard_count, hidden_part, 2 * width),
        "shard",
        scatter_dimension=0,
        tiled=False,
    )
    g_feed = lax.all_gather(g_feed, "heads", axis=0, tiled=False).reshape(hidden_own, 2 * width)
    g_up = g_feed[:, :width].T.astype(jnp.float32)
    g_down = g_feed[:, width:].astype(jnp.float32)

    own_grad_f = own_grad_rows.astype(jnp.float32)
    g_bias_down = jnp.sum(own_grad_f, axis=0)
    d_resid_norm, g_gain_two, g_shift_two = norm_two_back(d_normed_two)
    d_resid = own_grad_f + d_resid_norm
    d_branch = d_resid.astype(jnp.bfloat16)
    g_bias_out = jnp.sum(d_branch.astype(jnp.float32), axis=0)
    d_attended = dot_nt(d_branch, w_out).astype(jnp.bfloat16)
    d_sets = jnp.stack(
        [
            jnp.pad(
                d_attended[:, firsts[member] * HD : (firsts[member] + counts[member]) * HD],
                ((0, 0), (0, slot_width - counts[member] * HD)),
            )
            for member in range(team)
        ],
        axis=0,
    )
    d_flat = swap(d_sets, TEAM).reshape(group_tok, slot_width)
    g_out = dot_tn(attn_tok, d_branch)
    g_out = lax.psum_scatter(
        g_out.astype(jnp.bfloat16).reshape(shard_count * tensor_count, own_rows, width),
        OWNERS,
        scatter_dimension=0,
        tiled=False,
    )
    g_out = lax.psum(g_out, "heads").astype(jnp.float32)

    query_grad, key_grad, value_grad = attend_back(
        query_flat, key_flat, value_flat, d_flat, log_totals, bounds, prev_tok
    )
    spill = jnp.concatenate([key_grad[:prev_tok], value_grad[:prev_tok]], axis=1)
    later = from_behind(spill.astype(jnp.bfloat16), "shard", -1).astype(jnp.float32)
    later = jnp.pad(later, ((group_tok - prev_tok, 0), (0, 0)))
    own_grads = jnp.concatenate([key_grad[prev_tok:], value_grad[prev_tok:]], axis=1) + later
    d_projected = jnp.concatenate(
        [query_grad.astype(jnp.bfloat16), own_grads.astype(jnp.bfloat16)], axis=1
    )
    d_normed_part = dot_nt(d_projected, w_set)
    d_normed = team_sum(d_normed_part)
    g_attend = dot_tn(normed, d_projected)
    g_attend = sum_parts(
        g_attend.astype(jnp.bfloat16).reshape(
            shard_count, tensor_count * own_rows, 3 * slot_width
        ),
        "shard",
    )
    g_attend = g_attend.astype(jnp.bfloat16).reshape(1, tensor_count, own_rows, 3 * slot_width)
    g_attend = swap(
        jnp.broadcast_to(g_attend, (heads_count, *g_attend.shape[1:])).reshape(
            team, own_rows, 3 * slot_width
        ),
        TEAM,
    )
    g_attend = jnp.concatenate(
        [
            g_attend[member, :, part * slot_width : part * slot_width + counts[member] * HD]
            for part in range(3)
            for member in range(team)
        ],
        axis=1,
    ).astype(jnp.float32)

    d_sum = jnp.sum(d_projected.astype(jnp.float32), axis=0)

    def place_vector(vector):
        spread = jnp.zeros((width + tail_heads * HD,), jnp.float32)
        own_terms = jnp.where(column_valid, vector, 0)
        return lax.dynamic_update_slice_in_dim(spread, own_terms, my_first * HD, 0)[:width]

    g_bias_up_all = lax.dynamic_update_slice(
        jnp.zeros((shard_count, tensor_count, heads_count, hidden_part), jnp.float32),
        g_bias_up.reshape(shard_count, 1, 1, hidden_part),
        (0, tensor_idx, heads_idx, 0),
    ).reshape(-1)
    owners = shard_count * tensor_count
    terms = jnp.concatenate(
        [
            vector.reshape(owners, -1)
            for vector in (
                jnp.sum(d_normed_part * unit, axis=0),
                jnp.sum(d_normed_part, axis=0),
                place_vector(d_sum[:slot_width]),
                place_vector(d_sum[2 * slot_width :]),
                g_bias_out,
                g_gain_two,
                g_shift_two,
                g_bias_down,
                g_bias_up_all,
            )
        ],
        axis=1,
    )
    sums = jnp.sum(gather_parts(sum_parts(terms, OWNERS), "heads"), axis=0)
    (
        s_gain_one,
        s_shift_one,
        s_bias_query,
        s_bias_value,
        s_bias_out,
        s_gain_two,
        s_shift_two,
        s_bias_down,
    ) = (sums[member * own_rows : (member + 1) * own_rows] for member in range(8))
    s_bias_up = sums[8 * own_rows :]

    own_center = own_tok_f - jnp.mean(own_tok_f, axis=-1, keepdims=True)
    own_inverse = lax.rsqrt(jnp.mean(own_center * own_center, axis=-1, keepdims=True) + EPS)
    own_unit = own_center * own_inverse
    scaled = d_normed * gain_one
    tokens_grad = d_resid + own_inverse * (
        scaled
        - jnp.mean(scaled, axis=-1, keepdims=True)
        - own_unit * jnp.mean(scaled * own_unit, axis=-1, keepdims=True)
    )
    return (
        layer_out,
        tokens_grad,
        g_attend,
        g_out,
        g_up,
        g_down,
        s_gain_one,
        s_shift_one,
        s_bias_query,
        s_bias_value,
        s_bias_out,
        s_gain_two,
        s_shift_two,
        s_bias_up,
        s_bias_down,
    )


def solution(mesh):
    placed = (
        P(("shard", "heads", "tensor"), None),
        P(("shard", "heads"), None),
        P(),
        P(("shard", "tensor"), None),
        P(("shard", "tensor"), None),
        P(None, ("shard", "tensor")),
        P(("shard", "tensor"), None),
        P(("shard", "tensor")),
        P(("shard", "tensor")),
        P(("shard", "tensor")),
        P(("shard", "tensor")),
        P(("shard", "tensor")),
        P(("shard", "tensor")),
        P(("shard", "tensor")),
        P(("shard", "tensor")),
        P(("shard", "tensor")),
    )
    return jax.shard_map(
        shards,
        mesh=mesh,
        in_specs=placed,
        out_specs=(
            P(("shard", "heads", "tensor"), None),
            P(("shard", "heads", "tensor"), None),
            P(("shard", "tensor"), None),
            P(("shard", "tensor"), None),
            P(None, ("shard", "tensor")),
            P(("shard", "tensor"), None),
            P(("shard", "tensor")),
            P(("shard", "tensor")),
            P(("shard", "tensor")),
            P(("shard", "tensor")),
            P(("shard", "tensor")),
            P(("shard", "tensor")),
            P(("shard", "tensor")),
            P(("shard", "tensor")),
            P(("shard", "tensor")),
        ),
        check_vma=False,
    )
```
